32 devices in a mesh: tm: 8 (over z, x), lat: 4 (over y, core).
Axes of the slice: x: 2, y: 2, z: 4, core: 2. Of those that a mesh axis runs over, the one named last changes fastest.
Arguments:
- fields: bfloat16 [8, 720, 1440], P('tm', 'lat'), may hold values from -6 to 6
- legendre: bfloat16 [720, 720, 720], P('lat', 'tm'), may hold values from -0.21875 to 0.21875
- nugget: float32 [720, 720, 2], P('lat', 'tm'), may hold values from 0.2 to 2
- chosen: int32 [1024], replicated, may hold values from 0 to 1036799, as said below
Outputs:
- panels: bfloat16 [720, 720, 2, 1024], P('lat', 'tm')
The draws below stay inside these ranges and needn't reach their ends.
Inputs may be any that keep to these rules, and one draw needn't show every extreme that they name: `chosen`: distinct flat indices (l * 720 + m) 2 + c with l >= m and not c = 1 at m = 0.
All inputs are finite; a program needn't handle non-finite values.
Results may differ from the reference program's by a relative error of at most 0.028.
Values may be sent and summed in bfloat16 or wider, within the bound.
No kernel may reach another device: no remote copies, remote signals or barrier semaphores. Data moves between devices by JAX's collectives and lax.ppermute only.
A program may use at most 448 MiB of HBM per device.

```python
import math
import jax
import jax.numpy as jnp
from jax import lax

NLON = 1440
NLAT = 720
ORD = 720
DEG = 720
PANEL = 512
TIMES = 8
N_LAT = 4


def draw_chosen(key, part):
    flat = jnp.arange(DEG * ORD * 2, dtype=jnp.int32)
    comp = flat % 2
    order = flat // 2 % ORD
    degree = flat // (2 * ORD)
    valid = (degree >= order) & jnp.logical_not((order == 0) & (comp == 1))
    count = sum(((DEG - m) * 2 for m in range(ORD))) - DEG
    places = jnp.nonzero(valid, size=count)[0].astype(jnp.int32)
    order_perm = jax.random.permutation(jax.random.fold_in(key, 7), count)
    return places[order_perm[:2 * PANEL]].astype(jnp.int32)


def level_of(rng, extent, cuts, low, top_value):
    factor_of = 1.0
    for position, shards_of in cuts:
        draws = jax.random.uniform(jax.random.fold_in(jax.random.fold_in(rng, 6), position), (shards_of,), jnp.float32, low / len(cuts), top_value / len(cuts))
        factor_of = factor_of * jnp.repeat(jnp.exp(draws), extent[position] // shards_of).reshape((-1,) + (1,) * (len(extent) - 1 - position))
    return factor_of


def scatter_about(key, dims, deviation, bound, pieces=(), held_as=jnp.bfloat16):
    array = deviation * jax.random.normal(key, dims, jnp.float32)
    if pieces:
        array = array * level_of(key, dims, pieces, -0.22, 0.18)
    return jnp.clip(array, -bound, bound).astype(held_as)


def setup_inputs(seed: int = 0) -> dict:
    key_of = jax.random.split(jax.random.key(seed), 5)
    fields = scatter_about(key_of[0], (TIMES, NLAT, NLON), 1.0, 6.0, ((0, 8), (1, 4)))
    legendre = scatter_about(key_of[1], (NLAT, ORD, DEG), NLAT ** -0.5, 0.21875, ((0, 4), (1, 8)))
    nugget = jnp.clip(jnp.exp(math.log(2.0) - 2.3025851 * jax.random.uniform(key_of[2], (DEG, ORD, 2), jnp.float32) ** level_of(key_of[2], (DEG, ORD, 2), ((0, 4), (1, 8)), -0.2, 0.2)), 0.2, 2.0)
    chosen = draw_chosen(jax.random.fold_in(key_of[4], 71), 0)
    return {"fields": fields, "legendre": legendre, "nugget": nugget, "chosen": chosen}


HIGH = lax.Precision.HIGHEST

def basis_table(count_lon, count_ord):
    cols = jnp.arange(count_lon, dtype=jnp.int32)[:, None] * jnp.arange(count_ord, dtype=jnp.int32)[None, :]
    angle = (cols % count_lon).astype(jnp.float32) * (2.0 * math.pi / count_lon)
    scale = 1.0 / math.sqrt(count_lon)
    table = jnp.stack([jnp.cos(angle) * scale, -jnp.sin(angle) * scale], axis=2)
    return table.reshape(count_lon, 2 * count_ord).astype(jnp.bfloat16)

def reference(fields, legendre, nugget, chosen):
    times = fields.shape[0]
    basis = basis_table(NLON, ORD)
    spectra = jnp.dot(fields.reshape(-1, NLON).astype(jnp.float32), basis.astype(jnp.float32), preferred_element_type=jnp.float32)
    spectra = spectra.astype(jnp.bfloat16).reshape(times, NLAT, ORD, 2)
    keep = jnp.arange(DEG)[None, :] >= jnp.arange(ORD)[:, None]
    masked = jnp.where(keep[None], legendre, jnp.zeros_like(legendre))
    lat_block = NLAT // N_LAT
    total = jnp.zeros((DEG, times, ORD, 2), jnp.float32)
    for index in range(N_LAT):
        part_spec = spectra[:, index * lat_block:(index + 1) * lat_block].astype(jnp.float32)
        part_leg = masked[index * lat_block:(index + 1) * lat_block].astype(jnp.float32)
        partial_value = jnp.einsum('tjmc,jml->ltmc', part_spec, part_leg)
        total = total + partial_value.astype(jnp.bfloat16).astype(jnp.float32)
    coefs = total.astype(jnp.bfloat16)
    flat = jnp.transpose(coefs, (1, 0, 2, 3)).reshape(times, -1)
    picked = flat[:, chosen]
    nug_flat = nugget.reshape(-1)
    block = jnp.dot(picked.T.astype(jnp.float32), picked.astype(jnp.float32), preferred_element_type=jnp.float32) / times
    block = block + jnp.diag(nug_flat[chosen])
    b11 = block[:PANEL, :PANEL]
    b21 = block[PANEL:, :PANEL]
    b22 = block[PANEL:, PANEL:]
    eye = jnp.eye(PANEL, dtype=jnp.float32)
    l11 = jnp.linalg.cholesky(b11)
    inv11 = jax.scipy.linalg.solve_triangular(l11, eye, lower=True)
    l21 = jnp.dot(b21, inv11.T, precision=HIGH)
    l22 = jnp.linalg.cholesky(b22 - jnp.dot(l21, l21.T, precision=HIGH))
    inv22 = jax.scipy.linalg.solve_triangular(l22, eye, lower=True)
    ident = jnp.arange(DEG * ORD * 2, dtype=jnp.int32).reshape(DEG, ORD * 2)

    def one_degree(args):
        rows, index_row, nug_row = args
        cov = jnp.dot(rows.T.astype(jnp.float32), picked.astype(jnp.float32), preferred_element_type=jnp.float32) / times
        cov = cov + jnp.where(index_row[:, None] == chosen[None, :], nug_row[:, None], 0.0)
        first = jnp.dot(cov[:, :PANEL], inv11.T, precision=HIGH)
        second = jnp.dot(cov[:, PANEL:] - jnp.dot(first, l21.T, precision=HIGH), inv22.T, precision=HIGH)
        return jnp.concatenate([first, second], axis=1).astype(jnp.bfloat16)
    rows_by_deg = coefs.reshape(DEG, times, ORD * 2)
    out = lax.map(one_degree, (rows_by_deg, ident, nugget.reshape(DEG, ORD * 2)))
    return out.reshape(DEG, ORD, 2, 2 * PANEL)
```

```python
import functools
import math

import jax
import jax.numpy as jnp
import numpy as np
from jax import lax
from jax.experimental import pallas as pl
from jax.experimental.pallas import tpu as pltpu
from jax.sharding import PartitionSpec as P

LANE = 128
GROUP = 16
VMEM = 48 << 20
F32, BF16 = jnp.float32, jnp.bfloat16
NT = (((1,), (1,)), ((), ()))


def div_up(a, b):
    return -(-a // b)


def divisor(n, most):
    return max(d for d in range(1, most + 1) if n % d == 0)


def whole(a):
    return pl.BlockSpec(a.shape, lambda i, *_: (0,) * a.ndim)


def turn(r, n):
    x = (r - jnp.floor(r * (1.0 / n)) * n) * (4.0 / n)
    k = jnp.floor(x + 0.5)
    y = (x - k) * (math.pi / 2)
    z = y * y
    s = y * (1 + z * (-1 / 6 + z * (1 / 120 + z * (-1 / 5040 + z * (1 / 362880)))))
    c = 1 + z * (-1 / 2 + z * (1 / 24 + z * (-1 / 720 + z * (1 / 40320 - z * (1 / 3628800)))))
    odd = (k == 1) | (k == 3)
    cos = jnp.where(odd, s, c)
    sin = jnp.where(odd, c, s)
    cos = jnp.where((k == 1) | (k == 2), -cos, cos)
    sin = jnp.where((k == 2) | (k == 3), -sin, sin)
    return cos, sin


def spectra_kernel(n_lon, ords, rows, f_ref, o_ref, c_ref, s_ref):
    dest = pl.program_id(0)
    lats = f_ref.shape[0]
    tiles = rows // 8
    lane = lax.broadcasted_iota(jnp.int32, (tiles, 2 * LANE), 1)
    lane = jnp.where(lane < LANE, lane, LANE).astype(F32)
    first = (dest * ords + 8 * lax.broadcasted_iota(jnp.int32, (tiles, 2 * LANE), 0)).astype(F32)
    pc, ps = turn(first * lane, n_lon)
    few = lax.broadcasted_iota(jnp.int32, (8, 2 * LANE), 0).astype(F32)
    qc, qs = turn(few * lane[:1], n_lon)
    scale = 1.0 / math.sqrt(n_lon)
    for p in range(0, tiles, 2):
        both_c, both_s = [], []
        for i in (p, p + 1):
            both_c.append(pc[i : i + 1] * qc - ps[i : i + 1] * qs)
            both_s.append(ps[i : i + 1] * qc + pc[i : i + 1] * qs)
        cos = jnp.concatenate(both_c, axis=0)
        sin = jnp.concatenate(both_s, axis=0)
        rc, rs = cos[:, LANE:], sin[:, LANE:]
        c, s = cos[:, :LANE] * scale, sin[:, :LANE] * scale
        for a in range(div_up(n_lon, LANE)):
            width = min(LANE, n_lon - a * LANE)
            at = (slice(8 * p, 8 * p + 16), slice(a * LANE, a * LANE + width))
            c_ref[at] = c[:, :width].astype(BF16)
            s_ref[at] = (-s[:, :width]).astype(BF16)
            c, s = c * rc - s * rs, s * rc + c * rs
    f = f_ref[...]
    re = lax.dot_general(c_ref[...], f, NT, preferred_element_type=F32)
    im = lax.dot_general(s_ref[...], f, NT, preferred_element_type=F32)
    pad = jnp.zeros((rows, o_ref.shape[2] - 2 * lats), F32)
    o_ref[0] = jnp.concatenate([re, im, pad], axis=1).astype(BF16)


def spectra(fields, ords, dests):
    lats, n_lon = fields.shape
    rows = div_up(ords, GROUP) * GROUP
    lanes = div_up(2 * lats, LANE) * LANE
    return pl.pallas_call(
        functools.partial(spectra_kernel, n_lon, ords, rows),
        grid=(dests,),
        in_specs=[pl.BlockSpec((lats, n_lon), lambda i: (0, 0))],
        out_specs=pl.BlockSpec((1, rows, lanes), lambda i: (i, 0, 0)),
        out_shape=jax.ShapeDtypeStruct((dests, rows, lanes), BF16),
        scratch_shapes=[pltpu.VMEM((rows, n_lon), BF16), pltpu.VMEM((rows, n_lon), BF16)],
        compiler_params=pltpu.CompilerParams(vmem_limit_bytes=VMEM),
        name="spectra",
    )(fields)


def partial_kernel(
    dims, key_ref, keyn_ref, meta_ref, x_ref, leg_ref, nug_ref, perm_ref, sel_ref,
    keep_ref, send_ref, pick_ref, flat, turned, held, nugs,
):
    times, lats, ords, degs, blocks, deg_local, cols = dims
    step = pl.program_id(0)
    steps = pl.num_programs(0)
    width = 2 * times
    lanes = GROUP * width
    me, ord_start = meta_ref[0], meta_ref[1]

    @pl.when(step == 0)
    def _():
        held[...] = jnp.zeros_like(held)
        nugs[...] = jnp.zeros_like(nugs)

    x = x_ref[...].reshape(times * GROUP, x_ref.shape[2])
    x = jnp.dot(perm_ref[...], x, preferred_element_type=F32)
    re = x[:, :lats]
    im = x[:, lats : 2 * lats]
    deg = lax.broadcasted_iota(jnp.int32, (width, degs), 1)
    for r in range(GROUP):
        at = slice(times * r, times * r + times)
        row = jnp.concatenate([re[at], im[at]], axis=0).astype(BF16)
        y = jnp.dot(row, leg_ref[r], preferred_element_type=F32)
        order = step * GROUP + r
        least = jnp.where(order < ords, ord_start + order, degs)
        y = jnp.where(deg >= least, y, 0.0).astype(BF16).astype(F32)
        flat[width * r : width * (r + 1), :degs] = y
    turned[...] = flat[...].T
    for d in range(blocks):
        part = turned[deg_local * d : deg_local * (d + 1), :].astype(BF16)
        where = d ^ me

        @pl.when(where % 2 == 0)
        def _():
            keep_ref[where // 2] = part

        @pl.when(where % 2 == 1)
        def _():
            send_ref[where // 2] = part

    lane = lax.broadcasted_iota(jnp.int32, (1, lanes), 1)

    def pick(e, _):
        key = key_ref[e]
        k = key % cols
        place = key // cols
        c = place % 2
        l = place // 2 % degs
        m = place // (2 * degs) - step * GROUP
        low = (2 * m + c) * times
        row = turned[pl.ds(l, 1), :]
        held[pl.ds(k, 1), :] = jnp.where((lane >= low) & (lane < low + times), row, 0.0)
        return 0

    lax.fori_loop(meta_ref[3 + step], meta_ref[4 + step], pick, 0)

    @pl.when(step == steps - 1)
    def _():
        ords_lane = lax.broadcasted_iota(jnp.int32, (1, ords), 1)

        def pick_nugget(e, _):
            key = keyn_ref[e]
            k = key % cols
            place = key // cols
            c = place % 2
            m = place // 2 % ords
            row = nug_ref[place // (2 * ords), pl.ds(c, 1), :]
            nugs[pl.ds(k, 1), :ords] = jnp.where(ords_lane == m, row, 0.0)
            return 0

        lax.fori_loop(0, meta_ref[2], pick_nugget, 0)
        ones = jnp.ones((8, LANE), F32)
        for t in range(cols // LANE):
            at = slice(LANE * t, LANE * (t + 1))
            pick_ref[:times, t, :] = lax.dot_general(
                sel_ref[...], held[at, :].astype(BF16), NT, preferred_element_type=F32
            )
            got = lax.dot_general(
                ones, nugs[at, :], NT, preferred_element_type=F32, precision=lax.Precision.HIGHEST
            )
            pick_ref[times, pl.ds(t, 1), :] = got[:1]


def partials(moved, legendre, nugget, key, keyn, meta, blocks, cols):
    times, rows, width = moved.shape
    ords, lats, degs = legendre.shape
    deg_local = nugget.shape[0]
    lanes = GROUP * 2 * times
    steps = rows // GROUP
    n = times * GROUP
    perm = np.zeros((GROUP, times, times, GROUP), np.float32)
    for t in range(times):
        for m in range(GROUP):
            perm[m, t, t, m] = 1
    perm = jnp.asarray(perm.reshape(n, n), BF16)
    sel = jnp.asarray(np.tile(np.eye(times, dtype=np.float32), (1, 2 * GROUP)), BF16)
    half = jax.ShapeDtypeStruct((blocks // 2, deg_local, steps * lanes), BF16)
    half_spec = pl.BlockSpec((blocks // 2, deg_local, lanes), lambda i, *_: (0, 0, i))
    dims = (times, lats, ords, degs, blocks, deg_local, cols)
    assert ords <= LANE
    return pl.pallas_call(
        functools.partial(partial_kernel, dims),
        grid_spec=pltpu.PrefetchScalarGridSpec(
            num_scalar_prefetch=3,
            grid=(steps,),
            in_specs=[
                pl.BlockSpec((times, GROUP, width), lambda i, *_: (0, i, 0)),
                pl.BlockSpec((GROUP, lats, degs), lambda i, *_: (i, 0, 0)),
                whole(nugget),
                whole(perm),
                whole(sel),
            ],
            out_specs=[
                half_spec,
                half_spec,
                pl.BlockSpec((times + 1, cols // LANE, LANE), lambda i, *_: (0, 0, 0)),
            ],
            scratch_shapes=[
                pltpu.VMEM((lanes, div_up(degs, LANE) * LANE), F32),
                pltpu.VMEM((div_up(degs, LANE) * LANE, lanes), F32),
                pltpu.VMEM((cols, lanes), F32),
                pltpu.VMEM((cols, LANE), F32),
            ],
        ),
        out_shape=[half, half, jax.ShapeDtypeStruct((times + 1, cols // LANE, LANE), F32)],
        compiler_params=pltpu.CompilerParams(vmem_limit_bytes=VMEM),
        name="partials",
    )(key, keyn, meta, moved, legendre, nugget, perm, sel)


def factor_kernel(times, pick_ref, tri_ref, w_ref, ld_ref, held):
    tiles = pick_ref.shape[1]
    root = 1.0 / math.sqrt(times)
    u = [pick_ref[x].astype(BF16).astype(F32) * root for x in range(times)]
    nug = pick_ref[times]
    inv = 1.0 / nug
    un = [a * inv for a in u]
    pairs = [(a, b) for a in range(times) for b in range(a, times)]
    prod = jnp.concatenate([un[a] * u[b] for a, b in pairs], axis=0)
    sums = jnp.zeros((prod.shape[0], 2 * LANE), F32)
    for _ in range(3):
        part = prod.astype(BF16)
        sums = sums + jnp.dot(part, tri_ref[...], preferred_element_type=F32)
        prod = prod - part.astype(F32)
    row = lax.broadcasted_iota(jnp.int32, (tiles, LANE), 0)

    def shifted(v, by):
        return jnp.where(row >= by, pltpu.roll(v, by, axis=0), 0.0)

    g = {}
    for i, (a, b) in enumerate(pairs):
        at = slice(tiles * i, tiles * (i + 1))
        before = shifted(sums[at, LANE:], 1)
        by = 1
        while by < tiles:
            before = before + shifted(before, by)
            by *= 2
        g[a, b] = sums[at, :LANE] + before + (1.0 if a == b else 0.0)
    z = list(u)
    quad = jnp.zeros_like(nug)
    scaled = []
    for p in range(times):
        d = 1.0 / g[p, p]
        f = {a: g[p, a] * d for a in range(p + 1, times)}
        for a in range(p + 1, times):
            for b in range(a, times):
                g[a, b] = g[a, b] - f[a] * g[p, b]
            z[a] = z[a] - f[a] * z[p]
        quad = quad + z[p] * z[p] * d
        scaled.append((d, f))
    y = [None] * times
    for p in reversed(range(times)):
        d, f = scaled[p]
        y[p] = z[p] * d
        for b in range(p + 1, times):
            y[p] = y[p] - f[b] * y[b]
    diag = jnp.sqrt(nug + quad)
    over = root / diag
    for x in range(times):
        held[x] = y[x] * over
    zero = jnp.zeros((times, LANE), F32)
    for t in range(tiles):
        w = held[:, t, :]
        left = jnp.concatenate([w, zero], axis=1)
        right = jnp.concatenate([zero, w], axis=1)
        w_ref[4 * times * t : 4 * times * (t + 1)] = jnp.concatenate([left, left, right, right], axis=0).astype(BF16)
        ld_ref[2 * t : 2 * t + 2] = jnp.broadcast_to(diag[t : t + 1], (2, LANE))


def factor(picks):
    times, tiles = picks.shape[0] - 1, picks.shape[1]
    assert times % 8 == 0 and tiles == 8
    strict = np.triu(np.ones((LANE, LANE), np.float32), 1)
    tri = jnp.asarray(np.concatenate([strict, np.ones((LANE, LANE), np.float32)], axis=1), BF16)
    return pl.pallas_call(
        functools.partial(factor_kernel, times),
        out_shape=[
            jax.ShapeDtypeStruct((4 * times * tiles, 2 * LANE), BF16),
            jax.ShapeDtypeStruct((2 * tiles, LANE), F32),
        ],
        scratch_shapes=[pltpu.VMEM((times, tiles, LANE), F32)],
        compiler_params=pltpu.CompilerParams(vmem_limit_bytes=VMEM),
        name="factor",
    )(picks, tri)


def panel_kernel(dims, n_parts, key_ref, start_ref, *refs):
    times, ords, deg_local, block, inner = dims
    parts, (spread_ref, mask_ref, w_ref, ld_ref, o_ref, held) = refs[:n_parts], refs[n_parts:]
    step = pl.program_id(0)
    quads = div_up(ords, 2)
    per = LANE // (4 * times)
    kk = w_ref.shape[0]
    rows = mask_ref.shape[0]
    cols = rows // 2 * LANE

    @pl.when(step == 0)
    def _():
        total = sum(p[0].astype(F32) for p in parts).astype(BF16)
        for q in range(quads):
            w, s = divmod(q, per)
            held[q] = jnp.dot(
                total[:, LANE * w : LANE * (w + 1)],
                spread_ref[:, kk * s : kk * (s + 1)],
                preferred_element_type=F32,
            )

    mask = mask_ref[...]
    weights = w_ref[...]

    def some(i, _):
        lhs = []
        for u in range(inner):
            for q in range(quads):
                row = held[q, pl.ds(step * block + i * inner + u, 1), :]
                lhs.append(jnp.broadcast_to(row, (rows, kk)).astype(BF16) * mask)
        for at in range(0, len(lhs), 2 * quads):
            y = jnp.dot(
                jnp.concatenate(lhs[at : at + 2 * quads], axis=0), weights, preferred_element_type=F32
            ).astype(BF16)
            for j in range(at, min(at + 2 * quads, len(lhs))):
                u, q = divmod(j, quads)
                for h in range(2):
                    if 2 * q + h < ords:
                        o_ref[i * inner + u, 2 * q + h] = y[
                            rows * (j - at) : rows * (j - at + 1), LANE * h : LANE * (h + 1)
                        ]
        return 0

    lax.fori_loop(0, block // inner, some, 0)

    index = lax.broadcasted_iota(jnp.int32, (rows, LANE), 0)
    col = index // 2 * LANE + lax.broadcasted_iota(jnp.int32, (rows, LANE), 1)

    def chosen_row(e, _):
        key = key_ref[e]
        k = key % cols
        place = key // cols
        c = place % 2
        m = place // 2 % ords
        l = place // (2 * ords) - step * block
        old = o_ref[l, m].astype(F32)
        new = jnp.where(col < k, old, jnp.where(col == k, ld_ref[...], 0.0))
        o_ref[l, m] = jnp.where(index % 2 == c, new, old).astype(BF16)
        return 0

    lax.fori_loop(start_ref[step], start_ref[step + 1], chosen_row, 0)


def panels(key, starts, parts, weights, diag, dims):
    times, ords, deg_local, block, inner = dims
    quads = div_up(ords, 2)
    kk = weights.shape[0]
    rows = diag.shape[0]
    width = 4 * times
    lane = np.arange(LANE)[:, None]
    col = np.arange(LANE // width * kk)[None, :]
    spread = jnp.asarray(lane == col // kk * width + col % width, BF16)
    r = np.arange(rows)[:, None]
    z = np.arange(kk)[None, :]
    mask = jnp.asarray((r // 2 == z // width) & (r % 2 == z // times % 2), BF16)
    part_spec = pl.BlockSpec((1,) + parts[0].shape[1:], lambda i, *_: (0, 0, 0))
    out = pl.pallas_call(
        functools.partial(panel_kernel, dims, len(parts)),
        grid_spec=pltpu.PrefetchScalarGridSpec(
            num_scalar_prefetch=2,
            grid=(deg_local // block,),
            in_specs=[part_spec] * len(parts) + [whole(a) for a in (spread, mask, weights, diag)],
            out_specs=pl.BlockSpec((block, ords, rows, LANE), lambda i, *_: (i, 0, 0, 0)),
            scratch_shapes=[pltpu.VMEM((quads, deg_local, kk), F32)],
        ),
        out_shape=jax.ShapeDtypeStruct((deg_local, ords, rows, LANE), BF16),
        compiler_params=pltpu.CompilerParams(vmem_limit_bytes=VMEM),
        name="panels",
    )(key, starts, *parts, spread, mask, weights, diag)
    out = out.reshape(deg_local, ords, rows // 2, 2, LANE)
    return jnp.transpose(out, (0, 1, 3, 2, 4)).reshape(deg_local, ords, 2, rows // 2 * LANE)


def partner(axis, bit):
    size = lax.axis_size(axis)
    return [(i, i ^ bit) for i in range(size)]


def bits(axis):
    size = lax.axis_size(axis)
    return [1 << s for s in range(size.bit_length() - 1)]


def on_device(fields, legendre, nugget, chosen):
    ords, degs = legendre.shape[1], legendre.shape[2]
    deg_local = nugget.shape[0]
    tm, lat = lax.axis_size("tm"), lax.axis_size("lat")
    cols = chosen.shape[0]
    block = divisor(deg_local, 12)
    inner = divisor(block, 6)
    me = lax.axis_index("lat")
    ord_start = lax.axis_index("tm") * ords
    deg_start = me * deg_local

    sent = spectra(fields.reshape(-1, fields.shape[-1]), ords, tm)

    k = jnp.arange(cols, dtype=jnp.int32)
    deg = chosen // (2 * tm * ords)
    order = chosen // 2 % (tm * ords) - ord_start
    part = chosen % 2
    mine = (order >= 0) & (order < ords)
    here = mine & (deg >= deg_start) & (deg < deg_start + deg_local)
    none = jnp.int32(2**31 - 1)
    key = jnp.where(mine, ((order * degs + deg) * 2 + part) * cols + k, none)
    keyn = jnp.where(here, (((deg - deg_start) * ords + order) * 2 + part) * cols + k, none)
    both = jnp.sort(jnp.stack([key, keyn]), axis=1)
    steps = div_up(ords, GROUP)
    edge = jnp.arange(steps + 1, dtype=jnp.int32) * (GROUP * degs * 2 * cols)
    edge = edge.at[steps].set(none)
    groups = jnp.sum((key[None, :] < edge[:, None]).astype(jnp.int32), axis=1)
    edge = jnp.arange(deg_local // block + 1, dtype=jnp.int32) * (block * ords * 2 * cols)
    starts = jnp.sum((keyn[None, :] < edge[:, None]).astype(jnp.int32), axis=1)
    meta = jnp.concatenate([jnp.stack([me, ord_start, starts[-1]]).astype(jnp.int32), groups])

    moved = lax.all_to_all(sent, "tm", split_axis=0, concat_axis=0, tiled=True)
    keep, send, picks = partials(
        moved, jnp.transpose(legendre, (1, 0, 2)), jnp.transpose(nugget, (0, 2, 1)),
        both[0], both[1], meta, lat, cols,
    )
    times = moved.shape[0]
    parts = [keep, lax.ppermute(send, "lat", partner("lat", 1))]
    for bit in bits("lat")[1:]:
        out = sum(p[1::2].astype(F32) for p in parts).astype(BF16)
        parts = [p[0::2] if p.shape[0] > 2 else p for p in parts]
        parts.append(lax.ppermute(out, "lat", partner("lat", bit)))
    for axis in ("lat", "tm"):
        for bit in bits(axis):
            picks = picks + lax.ppermute(picks, axis, partner(axis, bit))
    weights, diag = factor(picks)
    return panels(both[1], starts, parts, weights, diag, (times, ords, deg_local, block, inner))


def solution(mesh):
    placed = (P("tm", "lat", None), P("lat", "tm", None), P("lat", "tm", None), P())
    return jax.shard_map(
        on_device, mesh=mesh, in_specs=placed, out_specs=P("lat", "tm", None, None), check_vma=False
    )
```

```python
import functools
import math

import jax
import jax.numpy as jnp
import numpy as np
from jax import lax
from jax.experimental import pallas as pl
from jax.experimental.pallas import tpu as pltpu
from jax.sharding import PartitionSpec as P

LANE = 128
ROWS = 16
GROUP = 16
VMEM = 48 << 20
F32, BF16 = jnp.float32, jnp.bfloat16
NT = (((1,), (1,)), ((), ()))


def div_up(a, b):
    return -(-a // b)


def shifts(cols, minor):
    part = (cols - 1).bit_length()
    return part, part + 1, part + 1 + (minor - 1).bit_length()


def make_key(k, part, minor, major, cols, size):
    at = shifts(cols, size)
    return k | (part << at[0]) | (minor << at[1]) | (major << at[2])


def split_key(key, cols, size):
    at = shifts(cols, size)
    low = lambda x, n: x & ((1 << n) - 1)
    return low(key, at[0]), low(key >> at[0], 1), low(key >> at[1], at[2] - at[1]), key >> at[2]


def divisor(n, most):
    return max(d for d in range(1, most + 1) if n % d == 0)


def whole(a):
    return pl.BlockSpec(a.shape, lambda i, *_: (0,) * a.ndim)


def turn(r, n):
    x = (r - jnp.floor(r * (1.0 / n)) * n) * (4.0 / n)
    k = jnp.floor(x + 0.5)
    y = (x - k) * (math.pi / 2)
    z = y * y
    s = y * (1 + z * (-1 / 6 + z * (1 / 120 + z * (-1 / 5040 + z * (1 / 362880)))))
    c = 1 + z * (-1 / 2 + z * (1 / 24 + z * (-1 / 720 + z * (1 / 40320 - z * (1 / 3628800)))))
    odd = (k == 1) | (k == 3)
    cos = jnp.where(odd, s, c)
    sin = jnp.where(odd, c, s)
    cos = jnp.where((k == 1) | (k == 2), -cos, cos)
    sin = jnp.where((k == 2) | (k == 3), -sin, sin)
    return cos, sin


def spectra_kernel(n_lon, ords, rows, f_ref, o_ref, c_ref, s_ref):
    dest = pl.program_id(0)
    lats = f_ref.shape[0]
    tiles = rows // 8
    lane = lax.broadcasted_iota(jnp.int32, (tiles, 2 * LANE), 1)
    lane = jnp.where(lane < LANE, lane, LANE).astype(F32)
    first = (dest * ords + 8 * lax.broadcasted_iota(jnp.int32, (tiles, 2 * LANE), 0)).astype(F32)
    pc, ps = turn(first * lane, n_lon)
    few = lax.broadcasted_iota(jnp.int32, (8, 2 * LANE), 0).astype(F32)
    qc, qs = turn(few * lane[:1], n_lon)
    scale = 1.0 / math.sqrt(n_lon)
    for p in range(0, tiles, 2):
        both_c, both_s = [], []
        for i in (p, p + 1):
            both_c.append(pc[i : i + 1] * qc - ps[i : i + 1] * qs)
            both_s.append(ps[i : i + 1] * qc + pc[i : i + 1] * qs)
        cos = jnp.concatenate(both_c, axis=0)
        sin = jnp.concatenate(both_s, axis=0)
        rc, rs = cos[:, LANE:], sin[:, LANE:]
        c, s = cos[:, :LANE] * scale, sin[:, :LANE] * scale
        for a in range(div_up(n_lon, LANE)):
            width = min(LANE, n_lon - a * LANE)
            at = (slice(8 * p, 8 * p + 16), slice(a * LANE, a * LANE + width))
            c_ref[at] = c[:, :width].astype(BF16)
            s_ref[at] = (-s[:, :width]).astype(BF16)
            c, s = c * rc - s * rs, s * rc + c * rs
    f = f_ref[...]
    re = lax.dot_general(c_ref[...], f, NT, preferred_element_type=F32)
    im = lax.dot_general(s_ref[...], f, NT, preferred_element_type=F32)
    pad = jnp.zeros((rows, o_ref.shape[2] - 2 * lats), F32)
    o_ref[0] = jnp.concatenate([re, im, pad], axis=1).astype(BF16)


def spectra(fields, ords, dests):
    lats, n_lon = fields.shape
    rows = div_up(ords, GROUP) * GROUP
    lanes = div_up(2 * lats, LANE) * LANE
    return pl.pallas_call(
        functools.partial(spectra_kernel, n_lon, ords, rows),
        grid=(dests,),
        in_specs=[pl.BlockSpec((lats, n_lon), lambda i: (0, 0))],
        out_specs=pl.BlockSpec((1, rows, lanes), lambda i: (i, 0, 0)),
        out_shape=jax.ShapeDtypeStruct((dests, rows, lanes), BF16),
        scratch_shapes=[pltpu.VMEM((rows, n_lon), BF16), pltpu.VMEM((rows, n_lon), BF16)],
        compiler_params=pltpu.CompilerParams(vmem_limit_bytes=VMEM),
        name="spectra",
    )(fields)


def partial_kernel(
    dims, key_ref, meta_ref, x_ref, leg_ref, nug_ref, perm_ref, sel_ref,
    keep_ref, send_ref, pick_ref, flat, turned, held,
):
    times, lats, ords, degs, blocks, deg_local, cols = dims
    step = pl.program_id(0)
    steps = pl.num_programs(0)
    width = 2 * times
    lanes = GROUP * width
    me, ord_start = meta_ref[0], meta_ref[1]

    @pl.when(step == 0)
    def _():
        held[...] = jnp.zeros_like(held)

    x = x_ref[...].reshape(times * GROUP, x_ref.shape[2])
    x = jnp.dot(perm_ref[...], x, preferred_element_type=F32)
    re = x[:, :lats]
    im = x[:, lats : 2 * lats]
    deg = lax.broadcasted_iota(jnp.int32, (width, degs), 1)
    def order_rows(r):
        at = slice(times * r, times * r + times)
        row = jnp.concatenate([re[at], im[at]], axis=0).astype(BF16)
        y = jnp.dot(row, leg_ref[r], preferred_element_type=F32)
        least = ord_start + step * GROUP + r
        flat[width * r : width * (r + 1), :degs] = jnp.where(deg >= least, y, 0.0).astype(BF16).astype(F32)

    full = ords - (div_up(ords, GROUP) - 1) * GROUP
    for r in range(full):
        order_rows(r)

    @pl.when(step < steps - 1)
    def _():
        for r in range(full, GROUP):
            order_rows(r)

    turned[...] = flat[...].T
    for d in range(blocks):
        part = turned[deg_local * d : deg_local * (d + 1), :].astype(BF16)
        where = d ^ me

        @pl.when(where % 2 == 0)
        def _():
            keep_ref[where // 2] = part

        @pl.when(where % 2 == 1)
        def _():
            send_ref[where // 2] = part

    lane = lax.broadcasted_iota(jnp.int32, (1, lanes), 1)

    def pick(e, _):
        k, c, l, m = split_key(key_ref[e], cols, degs)
        low = (2 * (m - step * GROUP) + c) * times
        row = turned[pl.ds(l, 1), :]
        held[pl.ds(k, 1), :] = jnp.where((lane >= low) & (lane < low + times), row, 0.0)
        return 0

    lax.fori_loop(meta_ref[2 + step], meta_ref[3 + step], pick, 0)

    @pl.when(step == steps - 1)
    def _():
        for t in range(cols // LANE):
            at = slice(LANE * t, LANE * (t + 1))
            pick_ref[:times, t, :] = lax.dot_general(
                sel_ref[...], held[at, :].astype(BF16), NT, preferred_element_type=F32
            )
        pick_ref[times] = nug_ref[...]


def partials(moved, legendre, nuggets, key, meta, blocks, cols):
    times, rows, width = moved.shape
    ords, lats, degs = legendre.shape
    deg_local = degs // blocks
    lanes = GROUP * 2 * times
    steps = rows // GROUP
    n = times * GROUP
    perm = np.zeros((GROUP, times, times, GROUP), np.float32)
    for t in range(times):
        for m in range(GROUP):
            perm[m, t, t, m] = 1
    perm = jnp.asarray(perm.reshape(n, n), BF16)
    sel = jnp.asarray(np.tile(np.eye(times, dtype=np.float32), (1, 2 * GROUP)), BF16)
    half = jax.ShapeDtypeStruct((blocks // 2, deg_local, steps * lanes), BF16)
    half_spec = pl.BlockSpec((blocks // 2, deg_local, lanes), lambda i, *_: (0, 0, i))
    dims = (times, lats, ords, degs, blocks, deg_local, cols)
    return pl.pallas_call(
        functools.partial(partial_kernel, dims),
        grid_spec=pltpu.PrefetchScalarGridSpec(
            num_scalar_prefetch=2,
            grid=(steps,),
            in_specs=[
                pl.BlockSpec((times, GROUP, width), lambda i, *_: (0, i, 0)),
                pl.BlockSpec((GROUP, lats, degs), lambda i, *_: (i, 0, 0)),
                whole(nuggets),
                whole(perm),
                whole(sel),
            ],
            out_specs=[
                half_spec,
                half_spec,
                pl.BlockSpec((times + 1, cols // LANE, LANE), lambda i, *_: (0, 0, 0)),
            ],
            scratch_shapes=[
                pltpu.VMEM((lanes, div_up(degs, LANE) * LANE), F32),
                pltpu.VMEM((div_up(degs, LANE) * LANE, lanes), F32),
                pltpu.VMEM((cols, lanes), F32),
            ],
        ),
        out_shape=[half, half, jax.ShapeDtypeStruct((times + 1, cols // LANE, LANE), F32)],
        compiler_params=pltpu.CompilerParams(vmem_limit_bytes=VMEM),
        name="partials",
    )(key, meta, moved, legendre, nuggets, perm, sel)


def nugget_kernel(dims, key_ref, count_ref, nug_ref, o_ref, held):
    ords, cols = dims
    held[...] = jnp.zeros_like(held)
    order = lax.broadcasted_iota(jnp.int32, (1, ords), 1)

    def pick(e, _):
        k, c, m, l = split_key(key_ref[e], cols, ords)
        row = nug_ref[l, pl.ds(c, 1), :]
        held[pl.ds(k, 1), :ords] = jnp.where(order == m, row, 0.0)
        return 0

    lax.fori_loop(0, count_ref[0], pick, 0)
    for t in range(cols // LANE):
        got = lax.dot_general(
            jnp.ones((8, LANE), F32),
            held[LANE * t : LANE * (t + 1), :],
            NT,
            preferred_element_type=F32,
            precision=lax.Precision.HIGHEST,
        )
        o_ref[pl.ds(t, 1), :] = got[:1]


def nuggets_of(key, count, nugget, cols):
    ords = nugget.shape[2]
    assert ords <= LANE
    return pl.pallas_call(
        functools.partial(nugget_kernel, (ords, cols)),
        grid_spec=pltpu.PrefetchScalarGridSpec(
            num_scalar_prefetch=2,
            grid=(1,),
            in_specs=[whole(nugget)],
            out_specs=pl.BlockSpec((cols // LANE, LANE), lambda i, *_: (0, 0)),
            scratch_shapes=[pltpu.VMEM((cols, LANE), F32)],
        ),
        out_shape=jax.ShapeDtypeStruct((cols // LANE, LANE), F32),
        compiler_params=pltpu.CompilerParams(vmem_limit_bytes=VMEM),
        name="nuggets",
    )(key, count, nugget)


def factor_kernel(times, pick_ref, tri_ref, w_ref, ld_ref, held):
    tiles = pick_ref.shape[1]
    root = 1.0 / math.sqrt(times)
    u = [pick_ref[x].astype(BF16).astype(F32) * root for x in range(times)]
    nug = pick_ref[times]
    inv = 1.0 / nug
    un = [a * inv for a in u]
    pairs = [(a, b) for a in range(times) for b in range(a, times)]
    prod = jnp.concatenate([un[a] * u[b] for a, b in pairs], axis=0)
    sums = jnp.zeros((prod.shape[0], 2 * LANE), F32)
    for _ in range(3):
        part = prod.astype(BF16)
        sums = sums + jnp.dot(part, tri_ref[...], preferred_element_type=F32)
        prod = prod - part.astype(F32)
    row = lax.broadcasted_iota(jnp.int32, (tiles, LANE), 0)

    def shifted(v, by):
        return jnp.where(row >= by, pltpu.roll(v, by, axis=0), 0.0)

    g = {}
    for i, (a, b) in enumerate(pairs):
        at = slice(tiles * i, tiles * (i + 1))
        before = shifted(sums[at, LANE:], 1)
        by = 1
        while by < tiles:
            before = before + shifted(before, by)
            by *= 2
        g[a, b] = sums[at, :LANE] + before + (1.0 if a == b else 0.0)
    z = list(u)
    quad = jnp.zeros_like(nug)
    scaled = []
    for p in range(times):
        d = 1.0 / g[p, p]
        f = {a: g[p, a] * d for a in range(p + 1, times)}
        for a in range(p + 1, times):
            for b in range(a, times):
                g[a, b] = g[a, b] - f[a] * g[p, b]
            z[a] = z[a] - f[a] * z[p]
        quad = quad + z[p] * z[p] * d
        scaled.append((d, f))
    y = [None] * times
    for p in reversed(range(times)):
        d, f = scaled[p]
        y[p] = z[p] * d
        for b in range(p + 1, times):
            y[p] = y[p] - f[b] * y[b]
    diag = jnp.sqrt(nug + quad)
    over = root / diag
    for x in range(times):
        held[x] = y[x] * over
    for t in range(tiles):
        at = slice(LANE * t, LANE * (t + 1))
        w_ref[:, at] = jnp.concatenate([held[:, t, :]] * ROWS, axis=0).astype(BF16)
        ld_ref[:, at] = jnp.broadcast_to(diag[t : t + 1], (2, LANE))


def factor(picks):
    times, tiles = picks.shape[0] - 1, picks.shape[1]
    assert times % 8 == 0 and tiles == 8
    strict = np.triu(np.ones((LANE, LANE), np.float32), 1)
    tri = jnp.asarray(np.concatenate([strict, np.ones((LANE, LANE), np.float32)], axis=1), BF16)
    return pl.pallas_call(
        functools.partial(factor_kernel, times),
        out_shape=[
            jax.ShapeDtypeStruct((ROWS * times, tiles * LANE), BF16),
            jax.ShapeDtypeStruct((2, tiles * LANE), F32),
        ],
        scratch_shapes=[pltpu.VMEM((times, tiles, LANE), F32)],
        compiler_params=pltpu.CompilerParams(vmem_limit_bytes=VMEM),
        name="factor",
    )(picks, tri)


def panel_kernel(dims, n_parts, key_ref, start_ref, *refs):
    times, ords, deg_local, block, merge = dims
    parts, (mask_ref, w_ref, ld_ref, out_ref, total, lhs, slots, sems) = refs[:n_parts], refs[n_parts:]
    steps = deg_local // block
    cols = ld_ref.shape[1]
    wide = ROWS * times
    windows, tail = divmod(2 * ords, ROWS)
    group = merge * windows * ROWS + (ROWS if tail else 0)

    total[...] = sum(p[0].astype(F32) for p in parts).astype(BF16).astype(F32)

    def out_copy(step):
        slot = lax.rem(step, 2)
        return pltpu.make_async_copy(slots.at[slot], out_ref.at[pl.ds(step * block, block)], sems.at[slot])

    def one_block(step, _):
        o_ref = slots.at[lax.rem(step, 2)]
        for v in range(block // merge):
            at = v * group
            rest = None
            for u in range(merge):
                row = total[pl.ds(step * block + v * merge + u, 1), :]
                for w in range(windows):
                    piece = jnp.broadcast_to(row[:, wide * w : wide * (w + 1)], (ROWS, wide)).astype(BF16)
                    lhs[at : at + ROWS, :] = piece * mask_ref[0]
                    at += ROWS
                if tail:
                    piece = jnp.broadcast_to(row[:, wide * windows : wide * (windows + 1)], (ROWS, wide))
                    piece = piece.astype(BF16) * mask_ref[1 + u]
                    rest = piece if rest is None else rest + piece
            if tail:
                lhs[at : at + ROWS, :] = rest

        @pl.when(step >= 2)
        def _():
            out_copy(step - 2).wait()

        for v in range(block // merge):
            y = jnp.dot(
                lhs[v * group : (v + 1) * group, :], w_ref[...], preferred_element_type=F32
            ).astype(BF16)
            size = windows * ROWS
            for u in range(merge):
                o_ref[v * merge + u, : size // 2] = y[u * size : (u + 1) * size].reshape(size // 2, 2, cols)
            if tail:
                last = y[merge * size :].reshape(ROWS // 2, 2, cols)
                for u in range(merge):
                    o_ref[v * merge + u, size // 2 :] = last[u * tail // 2 : (u + 1) * tail // 2]

        col = lax.broadcasted_iota(jnp.int32, (2, cols), 1)
        part = lax.broadcasted_iota(jnp.int32, (2, cols), 0)

        def chosen_row(e, _):
            k, c, m, l = split_key(key_ref[e], cols, ords)
            l = l - step * block
            old = o_ref[l, m].astype(F32)
            new = jnp.where(col < k, old, jnp.where(col == k, ld_ref[...], 0.0))
            o_ref[l, m] = jnp.where(part == c, new, old).astype(BF16)
            return 0

        lax.fori_loop(start_ref[step], start_ref[step + 1], chosen_row, 0)
        out_copy(step).start()
        return 0

    lax.fori_loop(0, steps, one_block, 0)
    for step in range(max(steps - 2, 0), steps):
        out_copy(step).wait()


def panels(key, starts, parts, weights, diag, dims):
    times, ords, deg_local, block = dims
    cols = diag.shape[1]
    wide = ROWS * times
    windows, tail = divmod(2 * ords, ROWS)
    merge = divisor(block, ROWS // tail if tail else 1)
    row = np.arange(ROWS)[:, None]
    of = np.arange(wide)[None, :] // times
    mask = [row == of] + [(row == tail * u + of) & (of < tail) for u in range(merge if tail else 0)]
    mask = jnp.asarray(np.stack(mask), BF16)
    part_spec = pl.BlockSpec((1,) + parts[0].shape[1:], lambda i, *_: (0, 0, 0))
    rows = block // merge * (merge * windows + (1 if tail else 0)) * ROWS
    return pl.pallas_call(
        functools.partial(panel_kernel, (times, ords, deg_local, block, merge), len(parts)),
        grid_spec=pltpu.PrefetchScalarGridSpec(
            num_scalar_prefetch=2,
            grid=(1,),
            in_specs=[part_spec] * len(parts) + [whole(a) for a in (mask, weights, diag)],
            out_specs=pl.BlockSpec(memory_space=pl.ANY),
            scratch_shapes=[
                pltpu.VMEM(parts[0].shape[1:], F32),
                pltpu.VMEM((rows, wide), BF16),
                pltpu.VMEM((2, block, ords, 2, cols), BF16),
                pltpu.SemaphoreType.DMA((2,)),
            ],
        ),
        out_shape=jax.ShapeDtypeStruct((deg_local, ords, 2, cols), BF16),
        compiler_params=pltpu.CompilerParams(vmem_limit_bytes=VMEM),
        name="panels",
    )(key, starts, *parts, mask, weights, diag)


def in_order(key):
    rank = jnp.sum((key[None, :] < key[:, None]).astype(jnp.int32), axis=1)
    at = jnp.arange(key.shape[0], dtype=jnp.int32)
    return jnp.sum(jnp.where(rank[None, :] == at[:, None], key[None, :], 0), axis=1)


def partner(axis, bit):
    size = lax.axis_size(axis)
    return [(i, i ^ bit) for i in range(size)]


def bits(axis):
    size = lax.axis_size(axis)
    return [1 << s for s in range(size.bit_length() - 1)]


def on_device(fields, legendre, nugget, chosen):
    ords, degs = legendre.shape[1], legendre.shape[2]
    deg_local = nugget.shape[0]
    tm, lat = lax.axis_size("tm"), lax.axis_size("lat")
    cols = chosen.shape[0]
    block = divisor(deg_local, 20)
    me = lax.axis_index("lat")
    ord_start = lax.axis_index("tm") * ords
    deg_start = me * deg_local

    sent = spectra(fields.reshape(-1, fields.shape[-1]), ords, tm)

    k = jnp.arange(cols, dtype=jnp.int32)
    deg = chosen // (2 * tm * ords)
    order = chosen // 2 % (tm * ords) - ord_start
    part = chosen % 2
    mine = (order >= 0) & (order < ords)
    here = mine & (deg >= deg_start) & (deg < deg_start + deg_local)
    none = jnp.int32(2**31 - 1)
    key = jnp.where(mine, make_key(k, part, deg, order, cols, degs), none)
    keyn = jnp.where(here, make_key(k, part, order, deg - deg_start, cols, ords), none)
    steps = div_up(ords, GROUP)
    edge = np.arange(steps + 1) * GROUP << shifts(cols, degs)[2]
    edge = jnp.asarray(np.minimum(edge, 2**31 - 1), jnp.int32)
    groups = jnp.sum((key[None, :] < edge[:, None]).astype(jnp.int32), axis=1)
    edge = jnp.asarray(np.arange(deg_local // block + 1) * block << shifts(cols, ords)[2], jnp.int32)
    starts = jnp.sum((keyn[None, :] < edge[:, None]).astype(jnp.int32), axis=1)
    meta = jnp.concatenate([jnp.stack([me, ord_start]).astype(jnp.int32), groups])
    key, keyn = in_order(key), in_order(keyn)

    nuggets = nuggets_of(keyn, starts[-1:], jnp.transpose(nugget, (0, 2, 1)), cols)
    moved = lax.all_to_all(sent, "tm", split_axis=0, concat_axis=0, tiled=True)
    keep, send, picks = partials(moved, jnp.transpose(legendre, (1, 0, 2)), nuggets, key, meta, lat, cols)
    times = moved.shape[0]
    picks = picks + lax.ppermute(picks, "lat", partner("lat", 1))
    send, picks = lax.optimization_barrier((send, picks))
    parts = [keep, lax.ppermute(send, "lat", partner("lat", 1))]
    for bit in bits("lat")[1:]:
        picks = picks + lax.ppermute(picks, "lat", partner("lat", bit))
        out = sum(p[1::2].astype(F32) for p in parts).astype(BF16)
        parts = [p[0::2] if p.shape[0] > 2 else p for p in parts]
        out, picks = lax.optimization_barrier((out, picks))
        parts.append(lax.ppermute(out, "lat", partner("lat", bit)))
    for bit in bits("tm"):
        picks = picks + lax.ppermute(picks, "tm", partner("tm", bit))
    weights, diag = factor(picks)
    return panels(keyn, starts, parts, weights, diag, (times, ords, deg_local, block))


def solution(mesh):
    placed = (P("tm", "lat", None), P("lat", "tm", None), P("lat", "tm", None), P())
    return jax.shard_map(
        on_device, mesh=mesh, in_specs=placed, out_specs=P("lat", "tm", None, None), check_vma=False
    )
```

```python
import functools
import math

import jax
import jax.numpy as jnp
import numpy as np
from jax import lax
from jax.experimental import pallas as pl
from jax.experimental.pallas import tpu as pltpu
from jax.sharding import PartitionSpec as P

LANE = 128
ROWS = 16
DESTS = 8
GROUP = 16
VMEM = 48 << 20
MOST = 58 << 20
F32, BF16 = jnp.float32, jnp.bfloat16
NT = (((1,), (1,)), ((), ()))


def div_up(a, b):
    return -(-a // b)


def shifts(cols, minor):
    part = (cols - 1).bit_length()
    return part, part + 1, part + 1 + (minor - 1).bit_length()


def make_key(k, part, minor, major, cols, size):
    at = shifts(cols, size)
    return k | (part << at[0]) | (minor << at[1]) | (major << at[2])


def split_key(key, cols, size):
    at = shifts(cols, size)
    low = lambda x, n: x & ((1 << n) - 1)
    return low(key, at[0]), low(key >> at[0], 1), low(key >> at[1], at[2] - at[1]), key >> at[2]


def divisor(n, most):
    return max(d for d in range(1, most + 1) if n % d == 0)


def whole(a):
    return pl.BlockSpec(a.shape, lambda i, *_: (0,) * a.ndim)


def turn(r, n):
    x = (r - jnp.floor(r * (1.0 / n)) * n) * (4.0 / n)
    k = jnp.floor(x + 0.5)
    y = (x - k) * (math.pi / 2)
    z = y * y
    s = y * (1 + z * (-1 / 6 + z * (1 / 120 + z * (-1 / 5040 + z * (1 / 362880)))))
    c = 1 + z * (-1 / 2 + z * (1 / 24 + z * (-1 / 720 + z * (1 / 40320 - z * (1 / 3628800)))))
    odd = (k == 1) | (k == 3)
    cos = jnp.where(odd, s, c)
    sin = jnp.where(odd, c, s)
    cos = jnp.where((k == 1) | (k == 2), -cos, cos)
    sin = jnp.where((k == 2) | (k == 3), -sin, sin)
    return cos, sin


def spectra_kernel(n_lon, ords, rows, f_hbm, o_ref, table, f_ref, sem):
    step = pl.program_id(0)
    per = o_ref.shape[0]
    lats = f_ref.shape[0]
    tiles = rows // 8

    @pl.when(step == 0)
    def _():
        pltpu.make_async_copy(f_hbm, f_ref, sem).start()

    shape = (per * tiles, 2 * LANE)
    lane = lax.broadcasted_iota(jnp.int32, shape, 1)
    lane = jnp.minimum(lane, LANE).astype(F32)
    tile = lax.broadcasted_iota(jnp.int32, shape, 0)
    of = sum((tile >= tiles * d).astype(jnp.int32) for d in range(1, per)) if per > 1 else 0
    first = ((step * per + of) * ords + 8 * (tile - tiles * of)).astype(F32)
    pc, ps = turn(first * lane, n_lon)
    few = lax.broadcasted_iota(jnp.int32, (8, 2 * LANE), 0).astype(F32)
    qc, qs = turn(few * lane[:1], n_lon)
    scale = 1.0 / math.sqrt(n_lon)
    for p in range(0, per * tiles, 2):
        both_c, both_s = [], []
        for i in (p, p + 1):
            both_c.append(pc[i : i + 1] * qc - ps[i : i + 1] * qs)
            both_s.append(ps[i : i + 1] * qc + pc[i : i + 1] * qs)
        cos = jnp.concatenate(both_c, axis=0)
        sin = jnp.concatenate(both_s, axis=0)
        rc, rs = cos[:, LANE:], sin[:, LANE:]
        c, s = cos[:, :LANE] * scale, sin[:, :LANE] * scale
        d, r = divmod(8 * p, rows)
        at_c, at_s = 2 * d * rows + r, (2 * d + 1) * rows + r
        for a in range(div_up(n_lon, LANE)):
            width = min(LANE, n_lon - a * LANE)
            at = slice(a * LANE, a * LANE + width)
            table[at_c : at_c + 16, at] = c[:, :width].astype(BF16)
            table[at_s : at_s + 16, at] = (-s[:, :width]).astype(BF16)
            c, s = c * rc - s * rs, s * rc + c * rs

    @pl.when(step == 0)
    def _():
        pltpu.make_async_copy(f_hbm, f_ref, sem).wait()

    pad = jnp.zeros((rows, o_ref.shape[2] - 2 * lats), F32)
    y = lax.dot_general(table[...], f_ref[...], NT, preferred_element_type=F32)
    for d in range(per):
        re = y[2 * d * rows : (2 * d + 1) * rows]
        im = y[(2 * d + 1) * rows : (2 * d + 2) * rows]
        o_ref[d] = jnp.concatenate([re, im, pad], axis=1).astype(BF16)


def spectra(fields, ords, dests):
    lats, n_lon = fields.shape
    rows = div_up(ords, GROUP) * GROUP
    lanes = div_up(2 * lats, LANE) * LANE
    per = divisor(dests, DESTS)
    return pl.pallas_call(
        functools.partial(spectra_kernel, n_lon, ords, rows),
        grid=(dests // per,),
        in_specs=[pl.BlockSpec(memory_space=pl.ANY)],
        out_specs=pl.BlockSpec((per, rows, lanes), lambda i: (i, 0, 0)),
        out_shape=jax.ShapeDtypeStruct((dests, rows, lanes), BF16),
        scratch_shapes=[
            pltpu.VMEM((2 * per * rows, n_lon), BF16),
            pltpu.VMEM((lats, n_lon), BF16),
            pltpu.SemaphoreType.DMA,
        ],
        compiler_params=pltpu.CompilerParams(vmem_limit_bytes=MOST),
        name="spectra",
    )(fields)


def partial_kernel(
    dims, key_ref, meta_ref, x_ref, leg_ref, nug_ref,
    keep_ref, send_ref, pick_ref, flat, turned, held,
):
    times, lats, ords, degs, blocks, deg_local, cols = dims
    step = pl.program_id(0)
    steps = pl.num_programs(0)
    width = 2 * times
    lanes = GROUP * width
    me, ord_start = meta_ref[0], meta_ref[1]

    @pl.when(step == 0)
    def _():
        held[...] = jnp.zeros_like(held)

    x = x_ref[...].reshape(times * GROUP, x_ref.shape[2])
    n = times * GROUP
    to = lax.broadcasted_iota(jnp.int32, (n, n), 0)
    of = lax.broadcasted_iota(jnp.int32, (n, n), 1)
    perm = (of == lax.rem(to, times) * GROUP + to // times).astype(F32).astype(BF16)
    x = jnp.dot(perm, x, preferred_element_type=F32)
    re = x[:, :lats]
    im = x[:, lats : 2 * lats]
    deg = lax.broadcasted_iota(jnp.int32, (width, degs), 1)
    def order_rows(r):
        at = slice(times * r, times * r + times)
        row = jnp.concatenate([re[at], im[at]], axis=0).astype(BF16)
        y = jnp.dot(row, leg_ref[r], preferred_element_type=F32)
        least = ord_start + step * GROUP + r
        flat[width * r : width * (r + 1), :degs] = jnp.where(deg >= least, y, 0.0).astype(BF16).astype(F32)

    full = ords - (div_up(ords, GROUP) - 1) * GROUP
    for r in range(full):
        order_rows(r)

    @pl.when(step < steps - 1)
    def _():
        for r in range(full, GROUP):
            order_rows(r)

    turned[...] = flat[...].T
    for d in range(blocks):
        part = turned[deg_local * d : deg_local * (d + 1), :].astype(BF16)
        where = d ^ me

        @pl.when(where % 2 == 0)
        def _():
            keep_ref[where // 2, :deg_local] = part

        @pl.when(where % 2 == 1)
        def _():
            send_ref[where // 2, :deg_local] = part

    lane = lax.broadcasted_iota(jnp.int32, (1, lanes), 1)

    def pick(e, _):
        k, c, l, m = split_key(key_ref[e], cols, degs)
        low = (2 * (m - step * GROUP) + c) * times
        row = turned[pl.ds(l, 1), :]
        held[pl.ds(k, 1), :] = jnp.where((lane >= low) & (lane < low + times), row, 0.0)
        return 0

    lax.fori_loop(meta_ref[2 + step], meta_ref[3 + step], pick, 0)

    @pl.when(step == steps - 1)
    def _():
        sel = lax.rem(lax.broadcasted_iota(jnp.int32, (times, lanes), 1), times)
        sel = (sel == lax.broadcasted_iota(jnp.int32, (times, lanes), 0)).astype(F32).astype(BF16)
        for t in range(cols // LANE):
            at = slice(LANE * t, LANE * (t + 1))
            pick_ref[:times, t, :] = lax.dot_general(
                sel, held[at, :].astype(BF16), NT, preferred_element_type=F32
            )
        pick_ref[times] = nug_ref[...]


def partials(moved, legendre, nuggets, key, meta, blocks, cols):
    times, rows, width = moved.shape
    ords, lats, degs = legendre.shape
    deg_local = degs // blocks
    lanes = GROUP * 2 * times
    steps = rows // GROUP
    held_rows = div_up(deg_local, 8) * 8
    half = jax.ShapeDtypeStruct((blocks // 2, held_rows, steps * lanes), BF16)
    half_spec = pl.BlockSpec((blocks // 2, held_rows, lanes), lambda i, *_: (0, 0, i))
    dims = (times, lats, ords, degs, blocks, deg_local, cols)
    return pl.pallas_call(
        functools.partial(partial_kernel, dims),
        grid_spec=pltpu.PrefetchScalarGridSpec(
            num_scalar_prefetch=2,
            grid=(steps,),
            in_specs=[
                pl.BlockSpec((times, GROUP, width), lambda i, *_: (0, i, 0)),
                pl.BlockSpec((GROUP, lats, degs), lambda i, *_: (i, 0, 0)),
                whole(nuggets),
            ],
            out_specs=[
                half_spec,
                half_spec,
                pl.BlockSpec((times + 1, cols // LANE, LANE), lambda i, *_: (0, 0, 0)),
            ],
            scratch_shapes=[
                pltpu.VMEM((lanes, div_up(degs, LANE) * LANE), F32),
                pltpu.VMEM((div_up(degs, LANE) * LANE, lanes), F32),
                pltpu.VMEM((cols, lanes), F32),
            ],
        ),
        out_shape=[half, half, jax.ShapeDtypeStruct((times + 1, cols // LANE, LANE), F32)],
        compiler_params=pltpu.CompilerParams(vmem_limit_bytes=VMEM),
        name="partials",
    )(key, meta, moved, legendre, nuggets)


def nugget_kernel(dims, key_ref, count_ref, nug_ref, o_ref, held):
    ords, cols = dims
    held[...] = jnp.zeros_like(held)
    order = lax.broadcasted_iota(jnp.int32, (1, ords), 1)

    def pick(e, _):
        k, c, m, l = split_key(key_ref[e], cols, ords)
        row = nug_ref[l, pl.ds(c, 1), :]
        held[pl.ds(k, 1), :ords] = jnp.where(order == m, row, 0.0)
        return 0

    lax.fori_loop(0, count_ref[0], pick, 0)
    for t in range(cols // LANE):
        got = lax.dot_general(
            jnp.ones((8, LANE), F32),
            held[LANE * t : LANE * (t + 1), :],
            NT,
            preferred_element_type=F32,
            precision=lax.Precision.HIGHEST,
        )
        o_ref[pl.ds(t, 1), :] = got[:1]


def nuggets_of(key, count, nugget, cols):
    ords = nugget.shape[2]
    assert ords <= LANE
    return pl.pallas_call(
        functools.partial(nugget_kernel, (ords, cols)),
        grid_spec=pltpu.PrefetchScalarGridSpec(
            num_scalar_prefetch=2,
            grid=(1,),
            in_specs=[whole(nugget)],
            out_specs=pl.BlockSpec((cols // LANE, LANE), lambda i, *_: (0, 0)),
            scratch_shapes=[pltpu.VMEM((cols, LANE), F32)],
        ),
        out_shape=jax.ShapeDtypeStruct((cols // LANE, LANE), F32),
        compiler_params=pltpu.CompilerParams(vmem_limit_bytes=VMEM),
        name="nuggets",
    )(key, count, nugget)


def factor_kernel(times, pick_ref, tri_ref, w_ref, ld_ref, held):
    tiles = pick_ref.shape[1]
    root = 1.0 / math.sqrt(times)
    u = [pick_ref[x].astype(BF16).astype(F32) * root for x in range(times)]
    nug = pick_ref[times]
    inv = 1.0 / nug
    un = [a * inv for a in u]
    pairs = [(a, b) for a in range(times) for b in range(a, times)]
    prod = jnp.concatenate([un[a] * u[b] for a, b in pairs], axis=0)
    sums = jnp.zeros((prod.shape[0], 2 * LANE), F32)
    for _ in range(3):
        part = prod.astype(BF16)
        sums = sums + jnp.dot(part, tri_ref[...], preferred_element_type=F32)
        prod = prod - part.astype(F32)
    row = lax.broadcasted_iota(jnp.int32, (tiles, LANE), 0)

    def shifted(v, by):
        return jnp.where(row >= by, pltpu.roll(v, by, axis=0), 0.0)

    g = {}
    for i, (a, b) in enumerate(pairs):
        at = slice(tiles * i, tiles * (i + 1))
        before = shifted(sums[at, LANE:], 1)
        by = 1
        while by < tiles:
            before = before + shifted(before, by)
            by *= 2
        g[a, b] = sums[at, :LANE] + before + (1.0 if a == b else 0.0)
    z = list(u)
    quad = jnp.zeros_like(nug)
    scaled = []
    for p in range(times):
        d = 1.0 / g[p, p]
        f = {a: g[p, a] * d for a in range(p + 1, times)}
        for a in range(p + 1, times):
            for b in range(a, times):
                g[a, b] = g[a, b] - f[a] * g[p, b]
            z[a] = z[a] - f[a] * z[p]
        quad = quad + z[p] * z[p] * d
        scaled.append((d, f))
    y = [None] * times
    for p in reversed(range(times)):
        d, f = scaled[p]
        y[p] = z[p] * d
        for b in range(p + 1, times):
            y[p] = y[p] - f[b] * y[b]
    diag = jnp.sqrt(nug + quad)
    over = root / diag
    for x in range(times):
        held[x] = y[x] * over
    for t in range(tiles):
        at = slice(LANE * t, LANE * (t + 1))
        w_ref[:, at] = jnp.concatenate([held[:, t, :]] * ROWS, axis=0).astype(BF16)
        ld_ref[:, at] = jnp.broadcast_to(diag[t : t + 1], (2, LANE))


def factor(picks):
    times, tiles = picks.shape[0] - 1, picks.shape[1]
    assert times % 8 == 0 and tiles == 8
    strict = np.triu(np.ones((LANE, LANE), np.float32), 1)
    tri = jnp.asarray(np.concatenate([strict, np.ones((LANE, LANE), np.float32)], axis=1), BF16)
    return pl.pallas_call(
        functools.partial(factor_kernel, times),
        out_shape=[
            jax.ShapeDtypeStruct((ROWS * times, tiles * LANE), BF16),
            jax.ShapeDtypeStruct((2, tiles * LANE), F32),
        ],
        scratch_shapes=[pltpu.VMEM((times, tiles, LANE), F32)],
        compiler_params=pltpu.CompilerParams(vmem_limit_bytes=VMEM),
        name="factor",
    )(picks, tri)


def blocks_of(count):
    if count % 20 == 0 and count >= 60:
        return 8, 20, 12, count // 20 - 1
    size = divisor(count, 20)
    assert count // size >= 3
    return size, size, size, count // size - 2


def block_edges(count):
    first, middle, last, n = blocks_of(count)
    return np.cumsum([0, first] + [middle] * n + [last])


def merged(size, tail):
    return divisor(size, ROWS // tail if tail else 1)


def panel_kernel(dims, n_parts, key_ref, start_ref, *refs):
    times, ords, deg_local = dims
    parts, (mask_ref, w_ref, ld_ref, out_ref, total, lhs, slots, sems) = refs[:n_parts], refs[n_parts:]
    cols = ld_ref.shape[1]
    wide = ROWS * times
    windows, tail = divmod(2 * ords, ROWS)
    first, middle, last, n_middle = blocks_of(deg_local)

    total[...] = sum(p[0].astype(F32) for p in parts).astype(BF16).astype(F32)

    def out_copy(b, low, size):
        slot = b % 2 if isinstance(b, int) else lax.rem(b, 2)
        return pltpu.make_async_copy(
            slots.at[slot, pl.ds(0, size)], out_ref.at[pl.ds(low, size)], sems.at[slot]
        )

    def middle_copy(i):
        return out_copy(1 + i, first + middle * i, middle)

    def do_block(b, low, size, wait):
        merge = merged(size, tail)
        group = merge * windows * ROWS + (ROWS if tail else 0)
        o_ref = slots.at[b % 2 if isinstance(b, int) else lax.rem(b, 2)]
        for v in range(size // merge):
            at = v * group
            rest = None
            for u in range(merge):
                row = total[pl.ds(low + v * merge + u, 1), :]
                for w in range(windows):
                    piece = jnp.broadcast_to(row[:, wide * w : wide * (w + 1)], (ROWS, wide)).astype(BF16)
                    lhs[at : at + ROWS, :] = piece * mask_ref[0]
                    at += ROWS
                if tail:
                    piece = jnp.broadcast_to(row[:, wide * windows : wide * (windows + 1)], (ROWS, wide))
                    piece = piece.astype(BF16) * mask_ref[1 + u]
                    rest = piece if rest is None else rest + piece
            if tail:
                lhs[at : at + ROWS, :] = rest

        wait()
        for v in range(size // merge):
            y = jnp.dot(
                lhs[v * group : (v + 1) * group, :], w_ref[...], preferred_element_type=F32
            ).astype(BF16)
            full = windows * ROWS
            for u in range(merge):
                o_ref[v * merge + u, : full // 2] = y[u * full : (u + 1) * full].reshape(full // 2, 2, cols)
            if tail:
                ends = y[merge * full :].reshape(ROWS // 2, 2, cols)
                for u in range(merge):
                    o_ref[v * merge + u, full // 2 :] = ends[u * tail // 2 : (u + 1) * tail // 2]

        col = lax.broadcasted_iota(jnp.int32, (2, cols), 1)
        part = lax.broadcasted_iota(jnp.int32, (2, cols), 0)

        def chosen_row(e, _):
            k, c, m, l = split_key(key_ref[e], cols, ords)
            l = l - low
            old = o_ref[l, m].astype(F32)
            new = jnp.where(col < k, old, jnp.where(col == k, ld_ref[...], 0.0))
            o_ref[l, m] = jnp.where(part == c, new, old).astype(BF16)
            return 0

        lax.fori_loop(start_ref[b], start_ref[b + 1], chosen_row, 0)
        out_copy(b, low, size).start()

    def middle_block(i, _):
        def wait():
            @pl.when(i == 1)
            def _():
                out_copy(0, 0, first).wait()

            @pl.when(i >= 2)
            def _():
                middle_copy(i - 2).wait()

        do_block(1 + i, first + middle * i, middle, wait)
        return 0

    do_block(0, 0, first, lambda: None)
    lax.fori_loop(0, n_middle, middle_block, 0)

    def wait_last():
        if n_middle >= 2:
            middle_copy(n_middle - 2).wait()
        else:
            out_copy(0, 0, first).wait()

    do_block(1 + n_middle, first + middle * n_middle, last, wait_last)
    middle_copy(n_middle - 1).wait()
    out_copy(1 + n_middle, first + middle * n_middle, last).wait()


def panels(key, starts, parts, weights, diag, dims):
    times, ords, deg_local = dims
    cols = diag.shape[1]
    wide = ROWS * times
    windows, tail = divmod(2 * ords, ROWS)
    sizes = blocks_of(deg_local)[:3]
    most = max(merged(size, tail) for size in sizes)
    row = np.arange(ROWS)[:, None]
    of = np.arange(wide)[None, :] // times
    mask = [row == of] + [(row == tail * u + of) & (of < tail) for u in range(most if tail else 0)]
    mask = jnp.asarray(np.stack(mask), BF16)
    part_spec = pl.BlockSpec((1,) + parts[0].shape[1:], lambda i, *_: (0, 0, 0))
    rows = max(size // merged(size, tail) * (merged(size, tail) * windows + (1 if tail else 0)) for size in sizes)
    return pl.pallas_call(
        functools.partial(panel_kernel, dims, len(parts)),
        grid_spec=pltpu.PrefetchScalarGridSpec(
            num_scalar_prefetch=2,
            grid=(1,),
            in_specs=[part_spec] * len(parts) + [whole(a) for a in (mask, weights, diag)],
            out_specs=pl.BlockSpec(memory_space=pl.ANY),
            scratch_shapes=[
                pltpu.VMEM(parts[0].shape[1:], F32),
                pltpu.VMEM((rows * ROWS, wide), BF16),
                pltpu.VMEM((2, max(sizes), ords, 2, cols), BF16),
                pltpu.SemaphoreType.DMA((2,)),
            ],
        ),
        out_shape=jax.ShapeDtypeStruct((deg_local, ords, 2, cols), BF16),
        compiler_params=pltpu.CompilerParams(vmem_limit_bytes=VMEM),
        name="panels",
    )(key, starts, *parts, mask, weights, diag)


def in_order(key):
    rank = jnp.sum((key[None, :] < key[:, None]).astype(jnp.int32), axis=1)
    at = jnp.arange(key.shape[0], dtype=jnp.int32)
    return jnp.sum(jnp.where(rank[None, :] == at[:, None], key[None, :], 0), axis=1)


def partner(axis, bit):
    size = lax.axis_size(axis)
    return [(i, i ^ bit) for i in range(size)]


def bits(axis):
    size = lax.axis_size(axis)
    return [1 << s for s in range(size.bit_length() - 1)]


def on_device(fields, legendre, nugget, chosen):
    ords, degs = legendre.shape[1], legendre.shape[2]
    deg_local = nugget.shape[0]
    tm, lat = lax.axis_size("tm"), lax.axis_size("lat")
    cols = chosen.shape[0]
    me = lax.axis_index("lat")
    ord_start = lax.axis_index("tm") * ords
    deg_start = me * deg_local

    sent = spectra(fields.reshape(-1, fields.shape[-1]), ords, tm)

    k = jnp.arange(cols, dtype=jnp.int32)
    deg = chosen // (2 * tm * ords)
    order = chosen // 2 % (tm * ords) - ord_start
    part = chosen % 2
    mine = (order >= 0) & (order < ords)
    here = mine & (deg >= deg_start) & (deg < deg_start + deg_local)
    none = jnp.int32(2**31 - 1)
    key = jnp.where(mine, make_key(k, part, deg, order, cols, degs), none)
    keyn = jnp.where(here, make_key(k, part, order, deg - deg_start, cols, ords), none)
    steps = div_up(ords, GROUP)
    edge = np.arange(steps + 1) * GROUP << shifts(cols, degs)[2]
    edge = jnp.asarray(np.minimum(edge, 2**31 - 1), jnp.int32)
    groups = jnp.sum((key[None, :] < edge[:, None]).astype(jnp.int32), axis=1)
    edge = jnp.asarray(block_edges(deg_local) << shifts(cols, ords)[2], jnp.int32)
    starts = jnp.sum((keyn[None, :] < edge[:, None]).astype(jnp.int32), axis=1)
    meta = jnp.concatenate([jnp.stack([me, ord_start]).astype(jnp.int32), groups])
    key, keyn = in_order(key), in_order(keyn)

    nuggets = nuggets_of(keyn, starts[-1:], jnp.transpose(nugget, (0, 2, 1)), cols)
    moved = lax.all_to_all(sent, "tm", split_axis=0, concat_axis=0, tiled=True)
    keep, send, picks = partials(moved, jnp.transpose(legendre, (1, 0, 2)), nuggets, key, meta, lat, cols)
    times = moved.shape[0]
    picks = picks + lax.ppermute(picks, "lat", partner("lat", 1))
    send, picks = lax.optimization_barrier((send, picks))
    parts = [keep, lax.ppermute(send, "lat", partner("lat", 1))]
    for bit in bits("lat")[1:]:
        picks = picks + lax.ppermute(picks, "lat", partner("lat", bit))
        out = sum(p[1::2].astype(F32) for p in parts).astype(BF16)
        parts = [p[0::2] if p.shape[0] > 2 else p for p in parts]
        out, picks = lax.optimization_barrier((out, picks))
        parts.append(lax.ppermute(out, "lat", partner("lat", bit)))
    for bit in bits("tm"):
        picks = picks + lax.ppermute(picks, "tm", partner("tm", bit))
    weights, diag = factor(picks)
    return panels(keyn, starts, parts, weights, diag, (times, ords, deg_local))


def solution(mesh):
    placed = (P("tm", "lat", None), P("lat", "tm", None), P("lat", "tm", None), P())
    return jax.shard_map(
        on_device, mesh=mesh, in_specs=placed, out_specs=P("lat", "tm", None, None), check_vma=False
    )
```

```python
import functools
import math

import jax
import jax.numpy as jnp
import numpy as np
from jax import lax
from jax.experimental import pallas as pl
from jax.experimental.pallas import tpu as pltpu
from jax.sharding import PartitionSpec as P

LANE = 128
ROWS = 16
GROUP = 32
VMEM = 48 << 20
MOST = 58 << 20
F32, BF16 = jnp.float32, jnp.bfloat16
NT = (((1,), (1,)), ((), ()))


def div_up(a, b):
    return -(-a // b)


def shifts(cols, minor):
    part = (cols - 1).bit_length()
    return part, part + 1, part + 1 + (minor - 1).bit_length()


def make_key(k, part, minor, major, cols, size):
    at = shifts(cols, size)
    return k | (part << at[0]) | (minor << at[1]) | (major << at[2])


def split_key(key, cols, size):
    at = shifts(cols, size)
    low = lambda x, n: x & ((1 << n) - 1)
    return low(key, at[0]), low(key >> at[0], 1), low(key >> at[1], at[2] - at[1]), key >> at[2]


def divisor(n, most):
    return max(d for d in range(1, most + 1) if n % d == 0)


def whole(a):
    return pl.BlockSpec(a.shape, lambda i, *_: (0,) * a.ndim)


def turn(r, n):
    x = (r - jnp.floor(r * (1.0 / n)) * n) * (4.0 / n)
    k = jnp.floor(x + 0.5)
    y = (x - k) * (math.pi / 2)
    z = y * y
    s = y * (1 + z * (-1 / 6 + z * (1 / 120 + z * (-1 / 5040 + z * (1 / 362880)))))
    c = 1 + z * (-1 / 2 + z * (1 / 24 + z * (-1 / 720 + z * (1 / 40320 - z * (1 / 3628800)))))
    odd = (k == 1) | (k == 3)
    cos = jnp.where(odd, s, c)
    sin = jnp.where(odd, c, s)
    cos = jnp.where((k == 1) | (k == 2), -cos, cos)
    sin = jnp.where((k == 2) | (k == 3), -sin, sin)
    return cos, sin


def spectra_kernel(n_lon, ords, rows, f_hbm, o_ref, table, f_ref, sem):
    per = o_ref.shape[0]
    lats = f_ref.shape[0]
    tiles = rows // 8
    fields_in = pltpu.make_async_copy(f_hbm, f_ref, sem)
    fields_in.start()

    shape = (per * tiles, 2 * LANE)
    lane = lax.broadcasted_iota(jnp.int32, shape, 1)
    lane = jnp.minimum(lane, LANE).astype(F32)
    tile = lax.broadcasted_iota(jnp.int32, shape, 0)
    of = sum((tile >= tiles * d).astype(jnp.int32) for d in range(1, per)) if per > 1 else 0
    first = (of * ords + 8 * (tile - tiles * of)).astype(F32)
    pc, ps = turn(first * lane, n_lon)
    few = lax.broadcasted_iota(jnp.int32, (8, 2 * LANE), 0).astype(F32)
    qc, qs = turn(few * lane[:1], n_lon)
    scale = 1.0 / math.sqrt(n_lon)

    def fill(p):
        both_c, both_s = [], []
        for i in (p, p + 1):
            both_c.append(pc[i : i + 1] * qc - ps[i : i + 1] * qs)
            both_s.append(ps[i : i + 1] * qc + pc[i : i + 1] * qs)
        cos = jnp.concatenate(both_c, axis=0)
        sin = jnp.concatenate(both_s, axis=0)
        rc, rs = cos[:, LANE:], sin[:, LANE:]
        c, s = cos[:, :LANE] * scale, sin[:, :LANE] * scale
        d, r = divmod(8 * p, rows)
        at_c, at_s = 2 * d * rows + r, (2 * d + 1) * rows + r
        for a in range(div_up(n_lon, LANE)):
            width = min(LANE, n_lon - a * LANE)
            at = slice(a * LANE, a * LANE + width)
            table[at_c : at_c + 16, at] = c[:, :width].astype(BF16)
            table[at_s : at_s + 16, at] = (-s[:, :width]).astype(BF16)
            c, s = c * rc - s * rs, s * rc + c * rs

    some = divisor(per, max(per // 2, 1))
    pad = jnp.zeros((rows, o_ref.shape[2] - 2 * lats), F32)
    for q in range(per // some + 1):
        if q < per // some:
            for p in range(q * some * tiles, (q + 1) * some * tiles, 2):
                fill(p)
        if q == 0:
            fields_in.wait()
            continue
        at = (q - 1) * some
        y = lax.dot_general(
            table[2 * at * rows : 2 * (at + some) * rows, :], f_ref[...], NT, preferred_element_type=F32
        )
        for d in range(some):
            re = y[2 * d * rows : (2 * d + 1) * rows]
            im = y[(2 * d + 1) * rows : (2 * d + 2) * rows]
            o_ref[at + d] = jnp.concatenate([re, im, pad], axis=1).astype(BF16)


def spectra(fields, ords, dests):
    lats, n_lon = fields.shape
    rows = div_up(ords, GROUP) * GROUP
    lanes = div_up(2 * lats, LANE) * LANE
    per = dests
    return pl.pallas_call(
        functools.partial(spectra_kernel, n_lon, ords, rows),
        in_specs=[pl.BlockSpec(memory_space=pl.ANY)],
        out_specs=pl.BlockSpec(memory_space=pltpu.VMEM),
        out_shape=jax.ShapeDtypeStruct((dests, rows, lanes), BF16),
        scratch_shapes=[
            pltpu.VMEM((2 * per * rows, n_lon), BF16),
            pltpu.VMEM((lats, n_lon), BF16),
            pltpu.SemaphoreType.DMA,
        ],
        compiler_params=pltpu.CompilerParams(vmem_limit_bytes=MOST),
        name="spectra",
    )(fields)


def partial_kernel(
    dims, key_ref, meta_ref, x_ref, leg_ref, nug_ref,
    keep_ref, send_ref, pick_ref, flat, turned, held,
):
    times, lats, ords, degs, blocks, deg_local, cols = dims
    step = pl.program_id(0)
    steps = pl.num_programs(0)
    width = 2 * times
    lanes = GROUP * width
    me, ord_start = meta_ref[0], meta_ref[1]

    @pl.when(step == 0)
    def _():
        held[...] = jnp.zeros_like(held)

    x = x_ref[...].reshape(times * GROUP, x_ref.shape[2])
    n = times * GROUP
    to = lax.broadcasted_iota(jnp.int32, (n, n), 0)
    of = lax.broadcasted_iota(jnp.int32, (n, n), 1)
    perm = (of == lax.rem(to, times) * GROUP + to // times).astype(F32).astype(BF16)
    x = jnp.dot(perm, x, preferred_element_type=F32)
    re = x[:, :lats]
    im = x[:, lats : 2 * lats]
    deg = lax.broadcasted_iota(jnp.int32, (width, degs), 1)
    def order_rows(r):
        at = slice(times * r, times * r + times)
        row = jnp.concatenate([re[at], im[at]], axis=0).astype(BF16)
        y = jnp.dot(row, leg_ref[r], preferred_element_type=F32)
        least = ord_start + step * GROUP + r
        flat[width * r : width * (r + 1), :degs] = jnp.where(deg >= least, y, 0.0).astype(BF16)

    full = ords - (div_up(ords, GROUP) - 1) * GROUP
    for r in range(full):
        order_rows(r)

    @pl.when(step < steps - 1)
    def _():
        for r in range(full, GROUP):
            order_rows(r)

    turned[...] = flat[...].T.astype(F32)
    for d in range(blocks):
        part = turned[deg_local * d : deg_local * (d + 1), :].astype(BF16)
        where = d ^ me

        @pl.when(where % 2 == 0)
        def _():
            keep_ref[where // 2, :deg_local] = part

        @pl.when(where % 2 == 1)
        def _():
            send_ref[where // 2, :deg_local] = part

    lane = lax.broadcasted_iota(jnp.int32, (1, lanes), 1)

    def pick(e, _):
        k, c, l, m = split_key(key_ref[e], cols, degs)
        low = (2 * (m - step * GROUP) + c) * times
        row = turned[pl.ds(l, 1), :]
        held[pl.ds(k, 1), :] = jnp.where((lane >= low) & (lane < low + times), row, 0.0)
        return 0

    lax.fori_loop(meta_ref[2 + step], meta_ref[3 + step], pick, 0)

    @pl.when(step == steps - 1)
    def _():
        sel = lax.rem(lax.broadcasted_iota(jnp.int32, (times, lanes), 1), times)
        sel = (sel == lax.broadcasted_iota(jnp.int32, (times, lanes), 0)).astype(F32).astype(BF16)
        for t in range(cols // LANE):
            at = slice(LANE * t, LANE * (t + 1))
            pick_ref[:times, t, :] = lax.dot_general(
                sel, held[at, :].astype(BF16), NT, preferred_element_type=F32
            )
        pick_ref[times] = nug_ref[...]


def partials(moved, legendre, nuggets, key, meta, blocks, cols):
    times, rows, width = moved.shape
    ords, lats, degs = legendre.shape
    deg_local = degs // blocks
    lanes = GROUP * 2 * times
    steps = rows // GROUP
    held_rows = div_up(deg_local, 8) * 8
    half = jax.ShapeDtypeStruct((blocks // 2, held_rows, steps * lanes), BF16)
    half_spec = pl.BlockSpec((blocks // 2, held_rows, lanes), lambda i, *_: (0, 0, i))
    dims = (times, lats, ords, degs, blocks, deg_local, cols)
    return pl.pallas_call(
        functools.partial(partial_kernel, dims),
        grid_spec=pltpu.PrefetchScalarGridSpec(
            num_scalar_prefetch=2,
            grid=(steps,),
            in_specs=[
                pl.BlockSpec((times, GROUP, width), lambda i, *_: (0, i, 0)),
                pl.BlockSpec((GROUP, lats, degs), lambda i, *_: (i, 0, 0)),
                whole(nuggets),
            ],
            out_specs=[
                half_spec,
                half_spec,
                pl.BlockSpec((times + 1, cols // LANE, LANE), lambda i, *_: (0, 0, 0)),
            ],
            scratch_shapes=[
                pltpu.VMEM((lanes, div_up(degs, LANE) * LANE), BF16),
                pltpu.VMEM((div_up(degs, LANE) * LANE, lanes), F32),
                pltpu.VMEM((cols, lanes), F32),
            ],
        ),
        out_shape=[half, half, jax.ShapeDtypeStruct((times + 1, cols // LANE, LANE), F32)],
        compiler_params=pltpu.CompilerParams(vmem_limit_bytes=VMEM),
        name="partials",
    )(key, meta, moved, legendre, nuggets)


def nugget_kernel(dims, key_ref, count_ref, nug_ref, o_ref, held):
    ords, cols = dims
    held[...] = jnp.zeros_like(held)
    order = lax.broadcasted_iota(jnp.int32, (1, ords), 1)

    def pick(e, _):
        k, c, m, l = split_key(key_ref[e], cols, ords)
        row = nug_ref[l, pl.ds(c, 1), :]
        held[pl.ds(k, 1), :ords] = jnp.where(order == m, row, 0.0)
        return 0

    lax.fori_loop(0, count_ref[0], pick, 0)
    for t in range(cols // LANE):
        got = lax.dot_general(
            jnp.ones((8, LANE), F32),
            held[LANE * t : LANE * (t + 1), :],
            NT,
            preferred_element_type=F32,
            precision=lax.Precision.HIGHEST,
        )
        o_ref[pl.ds(t, 1), :] = got[:1]


def nuggets_of(key, count, nugget, cols):
    ords = nugget.shape[2]
    assert ords <= LANE
    return pl.pallas_call(
        functools.partial(nugget_kernel, (ords, cols)),
        grid_spec=pltpu.PrefetchScalarGridSpec(
            num_scalar_prefetch=2,
            grid=(1,),
            in_specs=[whole(nugget)],
            out_specs=pl.BlockSpec((cols // LANE, LANE), lambda i, *_: (0, 0)),
            scratch_shapes=[pltpu.VMEM((cols, LANE), F32)],
        ),
        out_shape=jax.ShapeDtypeStruct((cols // LANE, LANE), F32),
        compiler_params=pltpu.CompilerParams(vmem_limit_bytes=VMEM),
        name="nuggets",
    )(key, count, nugget)


def factor_kernel(times, pick_ref, tri_ref, w_ref, ld_ref, held):
    tiles = pick_ref.shape[1]
    root = 1.0 / math.sqrt(times)
    u = [pick_ref[x].astype(BF16).astype(F32) * root for x in range(times)]
    nug = pick_ref[times]
    inv = 1.0 / nug
    un = [a * inv for a in u]
    pairs = [(a, b) for a in range(times) for b in range(a, times)]
    prod = jnp.concatenate([un[a] * u[b] for a, b in pairs], axis=0)
    sums = jnp.zeros((prod.shape[0], 2 * LANE), F32)
    for _ in range(3):
        part = prod.astype(BF16)
        sums = sums + jnp.dot(part, tri_ref[...], preferred_element_type=F32)
        prod = prod - part.astype(F32)
    row = lax.broadcasted_iota(jnp.int32, (tiles, LANE), 0)

    def shifted(v, by):
        return jnp.where(row >= by, pltpu.roll(v, by, axis=0), 0.0)

    g = {}
    for i, (a, b) in enumerate(pairs):
        at = slice(tiles * i, tiles * (i + 1))
        before = shifted(sums[at, LANE:], 1)
        by = 1
        while by < tiles:
            before = before + shifted(before, by)
            by *= 2
        g[a, b] = sums[at, :LANE] + before + (1.0 if a == b else 0.0)
    z = list(u)
    quad = jnp.zeros_like(nug)
    scaled = []
    for p in range(times):
        d = 1.0 / g[p, p]
        f = {a: g[p, a] * d for a in range(p + 1, times)}
        for a in range(p + 1, times):
            for b in range(a, times):
                g[a, b] = g[a, b] - f[a] * g[p, b]
            z[a] = z[a] - f[a] * z[p]
        quad = quad + z[p] * z[p] * d
        scaled.append((d, f))
    y = [None] * times
    for p in reversed(range(times)):
        d, f = scaled[p]
        y[p] = z[p] * d
        for b in range(p + 1, times):
            y[p] = y[p] - f[b] * y[b]
    diag = jnp.sqrt(nug + quad)
    over = root / diag
    for x in range(times):
        held[x] = y[x] * over
    for t in range(tiles):
        at = slice(LANE * t, LANE * (t + 1))
        w_ref[:, at] = jnp.concatenate([held[:, t, :]] * ROWS, axis=0).astype(BF16)
        ld_ref[:, at] = jnp.broadcast_to(diag[t : t + 1], (2, LANE))


def factor(picks):
    times, tiles = picks.shape[0] - 1, picks.shape[1]
    assert times % 8 == 0 and tiles == 8
    strict = np.triu(np.ones((LANE, LANE), np.float32), 1)
    tri = jnp.asarray(np.concatenate([strict, np.ones((LANE, LANE), np.float32)], axis=1), BF16)
    return pl.pallas_call(
        functools.partial(factor_kernel, times),
        out_shape=[
            jax.ShapeDtypeStruct((ROWS * times, tiles * LANE), BF16),
            jax.ShapeDtypeStruct((2, tiles * LANE), F32),
        ],
        scratch_shapes=[pltpu.VMEM((times, tiles, LANE), F32)],
        compiler_params=pltpu.CompilerParams(vmem_limit_bytes=VMEM),
        name="factor",
    )(picks, tri)


def blocks_of(count):
    if count % 20 == 0 and count >= 60:
        return 8, 20, 12, count // 20 - 1
    size = divisor(count, 20)
    assert count // size >= 3
    return size, size, size, count // size - 2


def block_edges(count):
    first, middle, last, n = blocks_of(count)
    return np.cumsum([0, first] + [middle] * n + [last])


def merged(size, tail):
    return divisor(size, ROWS // tail if tail else 1)


def panel_kernel(dims, n_parts, key_ref, start_ref, *refs):
    times, ords, deg_local = dims
    parts, (mask_ref, w_ref, ld_ref, out_ref, total, lhs, slots, sems) = refs[:n_parts], refs[n_parts:]
    cols = ld_ref.shape[1]
    wide = ROWS * times
    windows, tail = divmod(2 * ords, ROWS)
    first, middle, last, n_middle = blocks_of(deg_local)

    total[...] = sum(p[0].astype(F32) for p in parts).astype(BF16).astype(F32)

    def out_copy(b, low, size):
        slot = b % 2 if isinstance(b, int) else lax.rem(b, 2)
        return pltpu.make_async_copy(
            slots.at[slot, pl.ds(0, size)], out_ref.at[pl.ds(low, size)], sems.at[slot]
        )

    def middle_copy(i):
        return out_copy(1 + i, first + middle * i, middle)

    def do_block(b, low, size, wait):
        merge = merged(size, tail)
        group = merge * windows * ROWS + (ROWS if tail else 0)
        o_ref = slots.at[b % 2 if isinstance(b, int) else lax.rem(b, 2)]
        for v in range(size // merge):
            at = v * group
            rest = None
            for u in range(merge):
                row = total[pl.ds(low + v * merge + u, 1), :]
                for w in range(windows):
                    piece = jnp.broadcast_to(row[:, wide * w : wide * (w + 1)], (ROWS, wide)).astype(BF16)
                    lhs[at : at + ROWS, :] = piece * mask_ref[0]
                    at += ROWS
                if tail:
                    piece = jnp.broadcast_to(row[:, wide * windows : wide * (windows + 1)], (ROWS, wide))
                    piece = piece.astype(BF16) * mask_ref[1 + u]
                    rest = piece if rest is None else rest + piece
            if tail:
                lhs[at : at + ROWS, :] = rest

        wait()
        for v in range(size // merge):
            y = jnp.dot(
                lhs[v * group : (v + 1) * group, :], w_ref[...], preferred_element_type=F32
            ).astype(BF16)
            full = windows * ROWS
            for u in range(merge):
                o_ref[v * merge + u, : full // 2] = y[u * full : (u + 1) * full].reshape(full // 2, 2, cols)
            if tail:
                ends = y[merge * full :].reshape(ROWS // 2, 2, cols)
                for u in range(merge):
                    o_ref[v * merge + u, full // 2 :] = ends[u * tail // 2 : (u + 1) * tail // 2]

        col = lax.broadcasted_iota(jnp.int32, (2, cols), 1)
        part = lax.broadcasted_iota(jnp.int32, (2, cols), 0)

        def chosen_row(e, _):
            k, c, m, l = split_key(key_ref[e], cols, ords)
            l = l - low
            old = o_ref[l, m].astype(F32)
            new = jnp.where(col < k, old, jnp.where(col == k, ld_ref[...], 0.0))
            o_ref[l, m] = jnp.where(part == c, new, old).astype(BF16)
            return 0

        lax.fori_loop(start_ref[b], start_ref[b + 1], chosen_row, 0)
        out_copy(b, low, size).start()

    def middle_block(i, _):
        def wait():
            @pl.when(i == 1)
            def _():
                out_copy(0, 0, first).wait()

            @pl.when(i >= 2)
            def _():
                middle_copy(i - 2).wait()

        do_block(1 + i, first + middle * i, middle, wait)
        return 0

    do_block(0, 0, first, lambda: None)
    lax.fori_loop(0, n_middle, middle_block, 0)

    def wait_last():
        if n_middle >= 2:
            middle_copy(n_middle - 2).wait()
        else:
            out_copy(0, 0, first).wait()

    do_block(1 + n_middle, first + middle * n_middle, last, wait_last)
    middle_copy(n_middle - 1).wait()
    out_copy(1 + n_middle, first + middle * n_middle, last).wait()


def panels(key, starts, parts, weights, diag, dims):
    times, ords, deg_local = dims
    cols = diag.shape[1]
    wide = ROWS * times
    windows, tail = divmod(2 * ords, ROWS)
    sizes = blocks_of(deg_local)[:3]
    most = max(merged(size, tail) for size in sizes)
    row = np.arange(ROWS)[:, None]
    of = np.arange(wide)[None, :] // times
    mask = [row == of] + [(row == tail * u + of) & (of < tail) for u in range(most if tail else 0)]
    mask = jnp.asarray(np.stack(mask), BF16)
    part_spec = pl.BlockSpec((1,) + parts[0].shape[1:], lambda i, *_: (0, 0, 0))
    rows = max(size // merged(size, tail) * (merged(size, tail) * windows + (1 if tail else 0)) for size in sizes)
    return pl.pallas_call(
        functools.partial(panel_kernel, dims, len(parts)),
        grid_spec=pltpu.PrefetchScalarGridSpec(
            num_scalar_prefetch=2,
            grid=(1,),
            in_specs=[part_spec] * len(parts) + [whole(a) for a in (mask, weights, diag)],
            out_specs=pl.BlockSpec(memory_space=pl.ANY),
            scratch_shapes=[
                pltpu.VMEM(parts[0].shape[1:], F32),
                pltpu.VMEM((rows * ROWS, wide), BF16),
                pltpu.VMEM((2, max(sizes), ords, 2, cols), BF16),
                pltpu.SemaphoreType.DMA((2,)),
            ],
        ),
        out_shape=jax.ShapeDtypeStruct((deg_local, ords, 2, cols), BF16),
        compiler_params=pltpu.CompilerParams(vmem_limit_bytes=VMEM),
        name="panels",
    )(key, starts, *parts, mask, weights, diag)


def in_order(key):
    rank = jnp.sum((key[None, :] < key[:, None]).astype(jnp.int32), axis=1)
    at = jnp.arange(key.shape[0], dtype=jnp.int32)
    return jnp.sum(jnp.where(rank[None, :] == at[:, None], key[None, :], 0), axis=1)


def partner(axis, bit):
    size = lax.axis_size(axis)
    return [(i, i ^ bit) for i in range(size)]


def bits(axis):
    size = lax.axis_size(axis)
    return [1 << s for s in range(size.bit_length() - 1)]


def on_device(fields, legendre, nugget, chosen):
    ords, degs = legendre.shape[1], legendre.shape[2]
    deg_local = nugget.shape[0]
    tm, lat = lax.axis_size("tm"), lax.axis_size("lat")
    cols = chosen.shape[0]
    me = lax.axis_index("lat")
    ord_start = lax.axis_index("tm") * ords
    deg_start = me * deg_local

    sent = spectra(fields.reshape(-1, fields.shape[-1]), ords, tm)

    k = jnp.arange(cols, dtype=jnp.int32)
    deg = chosen // (2 * tm * ords)
    order = chosen // 2 % (tm * ords) - ord_start
    part = chosen % 2
    mine = (order >= 0) & (order < ords)
    here = mine & (deg >= deg_start) & (deg < deg_start + deg_local)
    none = jnp.int32(2**31 - 1)
    key = jnp.where(mine, make_key(k, part, deg, order, cols, degs), none)
    keyn = jnp.where(here, make_key(k, part, order, deg - deg_start, cols, ords), none)
    steps = div_up(ords, GROUP)
    edge = np.arange(steps + 1) * GROUP << shifts(cols, degs)[2]
    edge = jnp.asarray(np.minimum(edge, 2**31 - 1), jnp.int32)
    groups = jnp.sum((key[None, :] < edge[:, None]).astype(jnp.int32), axis=1)
    edge = jnp.asarray(block_edges(deg_local) << shifts(cols, ords)[2], jnp.int32)
    starts = jnp.sum((keyn[None, :] < edge[:, None]).astype(jnp.int32), axis=1)
    meta = jnp.concatenate([jnp.stack([me, ord_start]).astype(jnp.int32), groups])
    key, keyn = in_order(key), in_order(keyn)

    nuggets = nuggets_of(keyn, starts[-1:], jnp.transpose(nugget, (0, 2, 1)), cols)
    moved = lax.all_to_all(sent, "tm", split_axis=0, concat_axis=0, tiled=True)
    keep, send, picks = partials(moved, jnp.transpose(legendre, (1, 0, 2)), nuggets, key, meta, lat, cols)
    times = moved.shape[0]
    picks = picks + lax.ppermute(picks, "lat", partner("lat", 1))
    send, picks = lax.optimization_barrier((send, picks))
    parts = [keep, lax.ppermute(send, "lat", partner("lat", 1))]
    for bit in bits("lat")[1:]:
        picks = picks + lax.ppermute(picks, "lat", partner("lat", bit))
        out = sum(p[1::2].astype(F32) for p in parts).astype(BF16)
        parts = [p[0::2] if p.shape[0] > 2 else p for p in parts]
        out, picks = lax.optimization_barrier((out, picks))
        parts.append(lax.ppermute(out, "lat", partner("lat", bit)))
    for bit in bits("tm"):
        picks = picks + lax.ppermute(picks, "tm", partner("tm", bit))
    weights, diag = factor(picks)
    return panels(keyn, starts, parts, weights, diag, (times, ords, deg_local))


def solution(mesh):
    placed = (P("tm", "lat", None), P("lat", "tm", None), P("lat", "tm", None), P())
    return jax.shard_map(
        on_device, mesh=mesh, in_specs=placed, out_specs=P("lat", "tm", None, None), check_vma=False
    )
```
